256 devices in a mesh: dp: 16 (over y, x), tensor: 16 (over z, core).
Axes of the slice: x: 4, y: 4, z: 8, core: 2. Of those that a mesh axis runs over, the one named last changes fastest.
Arguments:
- inputs: bfloat16 [12288, 4096], P('dp', 'tensor'), may hold values from -6 to 6
- cotangent: bfloat16 [12288, 4096], P('dp', 'tensor'), may hold values from -0.059814453 to 0.059814453
- gate_pre: bfloat16 [12288, 18432], P('dp', 'tensor'), may hold values from -6 to 6
- up_pre: bfloat16 [12288, 18432], P('dp', 'tensor'), may hold values from -6 to 6
- down_weight: bfloat16 [18432, 4096], P('tensor'), may hold values from -0.046875 to 0.046875
- gate_a: bfloat16 [4096, 64], P('tensor'), may hold values from -0.09375 to 0.09375
- gate_b: bfloat16 [64, 18432], P(None, 'tensor'), may hold values from -0.75 to 0.75
- up_a: bfloat16 [4096, 64], P('tensor'), may hold values from -0.09375 to 0.09375
- up_b: bfloat16 [64, 18432], P(None, 'tensor'), may hold values from -0.75 to 0.75
- down_a: bfloat16 [18432, 64], P('tensor'), may hold values from -0.046875 to 0.046875
- down_adapter_second: bfloat16 [64, 4096], P(None, 'tensor'), may hold values from -0.75 to 0.75
Outputs:
- gate_first_gradient: float32 [4096, 64], P('tensor')
- gate_second_gradient: float32 [64, 18432], P(None, 'tensor')
- up_first_gradient: float32 [4096, 64], P('tensor')
- up_second_gradient: float32 [64, 18432], P(None, 'tensor')
- grad_down_a: float32 [18432, 64], P('tensor')
- down_second_gradient: float32 [64, 4096], P(None, 'tensor')
The draws below stay inside these ranges and needn't reach their ends.
All inputs are finite; a program needn't handle non-finite values.
Results may differ from the reference program's by a relative error of at most 0.005.
Values may be sent and summed in bfloat16 or wider, within the bound.
A program may use at most 64 MiB of HBM per device.

```python
import jax
import jax.numpy as jnp

D = 4096
FF = 18432
R = 64
TOKENS = 12288


def block_scale(rng, shape, split, low, largest):
    def one(axis_at, shards_of):
        steps = jax.random.uniform(jax.random.fold_in(jax.random.fold_in(rng, 6), axis_at), (shards_of,), jnp.float32, low / len(split), largest / len(split))
        return jnp.repeat(jnp.exp(steps), shape[axis_at] // shards_of).reshape((-1,) + (1,) * (len(shape) - axis_at - 1))

    gain = one(*split[0])
    for cut in split[1:]:
        gain = gain * one(*cut)
    return gain


def scatter_about(rng, shape, width, most, pieces=(), kind=jnp.bfloat16):
    drawn = jax.random.normal(rng, shape, jnp.float32) * width
    if len(pieces) > 0:
        drawn = block_scale(rng, shape, pieces, -0.22, 0.18) * drawn
    return jnp.clip(drawn, min=-most, max=most).astype(kind)


def setup_inputs(seed: int = 0) -> dict:
    seeds = jax.random.split(jax.random.key(seed), 12)
    inputs = scatter_about(seeds[0], (TOKENS, D), 1.0, 6.0, ((0, 16), (1, 16)))
    cotangent = scatter_about(seeds[1], (TOKENS, D), 0.01, 0.059814453, ((0, 16), (1, 16)))
    gate_pre = scatter_about(seeds[2], (TOKENS, FF), 1.0, 6.0, ((0, 16), (1, 16)))
    up_pre = scatter_about(seeds[3], (TOKENS, FF), 1.0, 6.0, ((0, 16), (1, 16)))
    down_weight = scatter_about(seeds[4], (FF, D), FF ** -0.5, 0.046875, ((0, 16),))
    gate_a = scatter_about(seeds[5], (D, R), D ** -0.5, 0.09375, ((0, 16),))
    gate_b = scatter_about(seeds[6], (R, FF), R ** -0.5, 0.75, ((1, 16),))
    up_a = scatter_about(seeds[7], (D, R), D ** -0.5, 0.09375, ((0, 16),))
    up_b = scatter_about(seeds[8], (R, FF), R ** -0.5, 0.75, ((1, 16),))
    down_a = scatter_about(seeds[9], (FF, R), FF ** -0.5, 0.046875, ((0, 16),))
    down_adapter_second = scatter_about(seeds[10], (R, D), R ** -0.5, 0.75, ((1, 16),))
    return {"inputs": inputs, "cotangent": cotangent, "gate_pre": gate_pre, "up_pre": up_pre, "down_weight": down_weight, "gate_a": gate_a, "gate_b": gate_b, "up_a": up_a, "up_b": up_b, "down_a": down_a, "down_adapter_second": down_adapter_second}


adapter_scale_factor = 2.0


def silu_parts(pre):
    sigma = jax.nn.sigmoid(pre)
    return pre * sigma, sigma * (1.0 + pre * (1.0 - sigma))


def matrix_multiply(left, right):
    return jnp.dot(left, right, preferred_element_type=jnp.float32)


def reference(inputs, cotangent, gate_pre, up_pre, down_weight, gate_a, gate_b, up_a, up_b, down_a, down_adapter_second):
    gate_wide = gate_pre.astype(jnp.float32)
    up_wide = up_pre.astype(jnp.float32)
    active, slope = silu_parts(gate_wide)
    hidden = (active * up_wide).astype(jnp.bfloat16)
    gate_reduced_rank = matrix_multiply(inputs, gate_a).astype(jnp.bfloat16)
    up_reduced_rank = matrix_multiply(inputs, up_a).astype(jnp.bfloat16)
    down_reduced_rank = matrix_multiply(hidden, down_a).astype(jnp.bfloat16)
    down_backward = (adapter_scale_factor * matrix_multiply(cotangent, down_adapter_second.T)).astype(jnp.bfloat16)
    hidden_grad = matrix_multiply(cotangent, down_weight.T) + matrix_multiply(down_backward, down_a.T)
    gate_gradient = (hidden_grad * up_wide * slope).astype(jnp.bfloat16)
    up_gradient = (hidden_grad * active).astype(jnp.bfloat16)
    gate_backward = matrix_multiply(gate_gradient, gate_b.T).astype(jnp.bfloat16)
    up_backward = matrix_multiply(up_gradient, up_b.T).astype(jnp.bfloat16)
    gate_second_gradient = adapter_scale_factor * matrix_multiply(gate_reduced_rank.T, gate_gradient)
    up_second_gradient = adapter_scale_factor * matrix_multiply(up_reduced_rank.T, up_gradient)
    gate_first_gradient = adapter_scale_factor * matrix_multiply(inputs.T, gate_backward)
    up_first_gradient = adapter_scale_factor * matrix_multiply(inputs.T, up_backward)
    grad_down_a = matrix_multiply(hidden.T, down_backward)
    down_second_gradient = adapter_scale_factor * matrix_multiply(down_reduced_rank.T, cotangent)
    return (gate_first_gradient, gate_second_gradient, up_first_gradient, up_second_gradient, grad_down_a, down_second_gradient)
```

```python
import functools

import jax
import jax.numpy as jnp
from jax import lax
from jax.experimental import pallas as pl
from jax.experimental.pallas import tpu as pltpu
from jax.sharding import PartitionSpec as P

MESH = pl.DeviceIdType.MESH
F32, BF16 = jnp.float32, jnp.bfloat16
CHUNKS = 4
SCALE = 2.0


def dot_nn(a, b):
    return jnp.dot(a, b, preferred_element_type=F32)


def dot_nt(a, b):
    return lax.dot_general(a, b, (((1,), (1,)), ((), ())), preferred_element_type=F32)


def pick(i, values):
    out = values[0]
    for k in range(1, len(values)):
        out = jnp.where(i == k, values[k], out)
    return out


def arrival_order(hops, chunks, ahead=3):
    events, sent, own = [], [], 0

    def run(event):
        events.append(event)
        if event[0] < hops:
            sent.append((event[0] + 1, event[1]))

    while own < min(ahead, chunks):
        run((0, own))
        own += 1
    at = 0
    while at < len(sent):
        run(sent[at])
        at += 1
        if at % 2 == 0 and own < chunks:
            run((0, own))
            own += 1
    return events


def main_kernel(
    nz, nd,
    x_hbm, c_hbm, g_hbm, u_hbm, w_hbm, ga_hbm, gb_hbm, ua_hbm, ub_hbm, da_hbm, ds_hbm,
    oa_hbm, ob_hbm, oc_hbm,
    cg, wv, gv, uv, act, usl, hid, xin, wf, wd, acc,
    lp, lpr, lsb, lrb, low, lowt,
    bp, bpr, bsb, brb, bk,
    gs, us, gda, dsec, gg, ug,
    sa, ra, ta, sb, rb, tb, sc, rc, tc,
    in_sem, w_sem, ring_recv, pair_recv, ring_send, pair_send, red_sem, dp_sem, out_sem,
):
    tokens, d_local = x_hbm.shape
    f_local = g_hbm.shape[1]
    rank = gb_hbm.shape[0]
    nt = 2 * nz
    hops = nz // 2
    rows = tokens // CHUNKS
    half = tokens // 2
    part = half // nz
    group = 16 // nd

    t_me = lax.axis_index("tensor")
    d_me = lax.axis_index("dp")
    z = t_me // 2
    c = t_me % 2
    way = 1 - 2 * c

    def at_z(offset):
        return lax.rem(z + offset + 2 * nz, nz)

    def block(offset, core):
        return 2 * at_z(offset) + core

    def remote(src, dst, send, recv, **where):
        return pltpu.make_async_remote_copy(
            src_ref=src, dst_ref=dst, send_sem=send, recv_sem=recv, device_id=where, device_id_type=MESH)

    def wait_bytes(ref, sem):
        pltpu.make_async_copy(ref, ref, sem).wait()

    loads = [
        pltpu.make_async_copy(c_hbm, cg.at[t_me], in_sem.at[0]),
        pltpu.make_async_copy(g_hbm, gv, in_sem.at[1]),
        pltpu.make_async_copy(u_hbm, uv, in_sem.at[2]),
        pltpu.make_async_copy(x_hbm, xin, in_sem.at[3]),
        pltpu.make_async_copy(ga_hbm, wd.at[0:rank], in_sem.at[4]),
        pltpu.make_async_copy(ua_hbm, wd.at[rank:2 * rank], in_sem.at[5]),
        pltpu.make_async_copy(ds_hbm, wd.at[3 * rank:4 * rank], in_sem.at[6]),
        pltpu.make_async_copy(gb_hbm, wf.at[0:rank], in_sem.at[7]),
        pltpu.make_async_copy(ub_hbm, wf.at[2 * rank:3 * rank], in_sem.at[8]),
        pltpu.make_async_copy(da_hbm, wf.at[4 * rank:5 * rank], in_sem.at[9]),
    ]
    for copy in loads:
        copy.start()
    w_loads = [
        pltpu.make_async_copy(w_hbm.at[:, k * d_local:(k + 1) * d_local], wv.at[k], w_sem) for k in range(nt)
    ]
    for copy in w_loads:
        copy.start()

    barrier = pltpu.get_barrier_semaphore()
    for k in range(1, nz):
        pl.semaphore_signal(barrier, inc=1, device_id={"tensor": block(k, c)}, device_id_type=MESH)
    pl.semaphore_signal(barrier, inc=1, device_id={"tensor": 2 * z + 1 - c}, device_id_type=MESH)
    for k in range(1, nd):
        pl.semaphore_signal(barrier, inc=1, device_id={"dp": lax.rem(d_me + k, nd)}, device_id_type=MESH)

    zeros = jnp.zeros((rank, f_local), BF16)
    wf[rank:2 * rank] = zeros
    wf[3 * rank:4 * rank] = zeros
    wf[5 * rank:6 * rank] = zeros
    wd[2 * rank:3 * rank] = jnp.zeros((rank, d_local), BF16)
    for r in range(4):
        sa[4 * r + 3, :, d_local:] = jnp.zeros((16, sa.shape[2] - d_local), BF16)
        for k in (1, 3):
            sb[4 * r + k, :, f_local - 640:] = jnp.zeros((16, 1280 - f_local), BF16)
    gs[...] = jnp.zeros_like(gs)
    us[...] = jnp.zeros_like(us)

    loads[0].wait()
    pl.semaphore_wait(barrier, nz + nd - 1)

    def piece(owner, core, q):
        return cg.at[block(owner, core), q * rows:(q + 1) * rows]

    def ring_slot(hop, down):
        return 2 * (hop - 1) + down

    def arrivals(hop):
        if hop == hops:
            return [(2 * (hops - 1), hops)]
        return [(ring_slot(hop, 0), -hop), (ring_slot(hop, 1), hop)]

    def pass_on(hop, q):
        if hop + 1 < hops:
            for down, step in ((0, 1), (1, -1)):
                src = piece(-step * hop, c, q)
                remote(src, src, ring_send, ring_recv.at[ring_slot(hop + 1, down), q],
                       tensor=block(step, c)).start()
        elif hop + 1 == hops:
            src = piece(-way * hop, c, q)
            remote(src, src, ring_send, ring_recv.at[2 * (hops - 1), q], tensor=block(way, c)).start()
        slots = [(0, 0)] if hop == 0 else [(s + 1, o) for s, o in arrivals(hop)]
        for slot, offset in slots:
            src = piece(offset, c, q)
            remote(src, src, pair_send, pair_recv.at[slot, q], tensor=2 * z + 1 - c).start()
        return [(slot, offset, q) for slot, offset in slots]

    def multiply(items):
        if not items:
            return
        blocks = [b for b, _ in items]
        qs = [q for _, q in items]

        def body(i, carry):
            b, q = pick(i, blocks), pick(i, qs)
            at = pl.multiple_of(q * rows, 16)
            acc[q] += dot_nt(cg[b, pl.ds(at, rows)], wv[b])
            return carry

        lax.fori_loop(0, len(items), body, 0)

    def prepare(q):
        def body(i, carry):
            at = pl.multiple_of(q * rows + i * 16, 16)
            g = gv[pl.ds(at, 16)].astype(F32)
            u = uv[pl.ds(at, 16)].astype(F32)
            s = 0.5 * jnp.tanh(0.5 * g) + 0.5
            a = g * s
            inner = pl.multiple_of(i * 16, 16)
            act[q, pl.ds(inner, 16)] = a
            usl[q, pl.ds(inner, 16)] = u * (s * (1.0 + (g - a)))
            hid[pl.ds(at, 16)] = (a * u).astype(BF16)
            return carry

        lax.fori_loop(0, rows // 16, body, 0)
        acc[q] = jnp.zeros((rows, f_local), F32)
        here = slice(q * rows, (q + 1) * rows)
        lp[here, :2 * rank] = dot_nt(xin[here], wd[:2 * rank])
        own = cg[t_me, q * rows:(q + 1) * rows]
        lp[here, 2 * rank:] = dot_nt(hid[here], wf[4 * rank:6 * rank]) + SCALE * dot_nt(own, wd[2 * rank:4 * rank])

    def z_steps(full, recv, out_b, in_b, result, base):
        mine = pl.ds(pl.multiple_of(c * half, 16), half)
        other = pl.ds(pl.multiple_of((1 - c) * half, 16), half)
        slice_rows = pl.ds(pl.multiple_of(c * half + z * part, 16), part)

        def exchange():
            remote(full.at[other], recv, red_sem.at[base], red_sem.at[base + 1], tensor=2 * z + 1 - c).start()

        def scatter():
            wait_bytes(recv, red_sem.at[base + 1])
            recv[...] += full[mine]
            for k in range(nz):
                out_b[k] = recv[k * part:(k + 1) * part].astype(BF16)
            for k in range(1, nz):
                to = at_z(k)
                remote(out_b.at[to], in_b.at[k - 1], red_sem.at[base + 2], red_sem.at[base + 3],
                       tensor=2 * to + c).start()

        def gather():
            wait_bytes(in_b, red_sem.at[base + 3])
            total = recv[pl.ds(pl.multiple_of(z * part, 16), part)]
            for k in range(nz - 1):
                total += in_b[k].astype(F32)
            result[slice_rows] = total.astype(BF16)
            for k in range(1, nz):
                remote(result.at[slice_rows], result.at[slice_rows], red_sem.at[base + 4], red_sem.at[base + 5],
                       tensor=block(k, c)).start()

        def share():
            wait_bytes(result.at[0:(nz - 1) * part], red_sem.at[base + 5])
            remote(result.at[mine], result.at[mine], red_sem.at[base + 6], red_sem.at[base + 7],
                   tensor=2 * z + 1 - c).start()

        def finish():
            wait_bytes(result.at[0:half], red_sem.at[base + 7])

        def drain():
            wait_bytes(recv, red_sem.at[base])
            wait_bytes(in_b, red_sem.at[base + 2])
            wait_bytes(result.at[0:(nz - 1) * part], red_sem.at[base + 4])
            wait_bytes(result.at[0:half], red_sem.at[base + 6])

        return exchange, scatter, gather, share, finish, drain

    def dp_steps(out_b, in_b, total_b, result, base):
        def scatter():
            for k in range(1, nd):
                to = lax.rem(d_me + k, nd)
                remote(out_b.at[pl.ds(to * group, group)], in_b.at[k - 1], dp_sem.at[base], dp_sem.at[base + 1],
                       dp=to).start()

        def gather():
            wait_bytes(in_b, dp_sem.at[base + 1])
            total = out_b[pl.ds(d_me * group, group)].astype(F32)
            for k in range(nd - 1):
                total += in_b[k].astype(F32)
            total_b[...] = total.astype(BF16)
            place = result.at[pl.ds(d_me * group, group)]
            for k in range(1, nd):
                remote(total_b, place, dp_sem.at[base + 2], dp_sem.at[base + 3], dp=lax.rem(d_me + k, nd)).start()
            pltpu.make_async_copy(total_b, place, out_sem.at[base // 4]).start()

        def finish():
            place = result.at[pl.ds(d_me * group, group)]
            pltpu.make_async_copy(total_b, place, out_sem.at[base // 4]).wait()
            wait_bytes(result.at[0:(nd - 1) * group], dp_sem.at[base + 3])
            wait_bytes(in_b, dp_sem.at[base])
            wait_bytes(result.at[0:(nd - 1) * group], dp_sem.at[base + 2])

        return scatter, gather, finish

    lows = z_steps(lp, lpr, lsb, lrb, low, 0)
    backs = z_steps(bp, bpr, bsb, brb, bk, 8)
    first_dp = dp_steps(sa, ra, ta, oa_hbm, 0)
    second_dp = dp_steps(sb, rb, tb, ob_hbm, 4)
    third_dp = dp_steps(sc, rc, tc, oc_hbm, 8)

    def use_lows():
        lows[4]()
        for q in range(CHUNKS):
            lowt[q] = jnp.transpose(low[q * rows:(q + 1) * rows].astype(F32)).astype(BF16)
        gda[...] = jnp.zeros_like(gda)
        dsec[...] = jnp.zeros_like(dsec)

        def body(q, carry):
            at = pl.ds(pl.multiple_of(q * rows, 16), rows)
            gda[...] += dot_nn(lowt[q, 3 * rank:], hid[at])
            dsec[...] += dot_nn(lowt[q, 2 * rank:3 * rank], cg[t_me, at])
            return carry

        lax.fori_loop(0, CHUNKS, body, 0)
        third = f_local // 3
        for r in range(4):
            at = slice(16 * r, 16 * r + 16)
            for k in range(3):
                sa[4 * r + k] = gda[at, k * third:(k + 1) * third].astype(BF16)
            sa[4 * r + 3, :, :d_local] = (SCALE * dsec[at]).astype(BF16)
        first_dp[0]()

    def post(q):
        lowq = low[q * rows:(q + 1) * rows, 2 * rank:]
        width = f_local // 3

        def body(i, carry):
            cols = pl.ds(pl.multiple_of(i * width, 128), width)
            grad = acc[q, :, cols] + dot_nn(lowq, wf[3 * rank:5 * rank, cols])
            gg[:, cols] = (grad * usl[q, :, cols]).astype(BF16)
            ug[:, cols] = (grad * act[q, :, cols]).astype(BF16)
            return carry

        lax.fori_loop(0, 3, body, 0)
        bp[q * rows:(q + 1) * rows] = dot_nt(gg[...], wf[:2 * rank]) + dot_nt(ug[...], wf[rank:3 * rank])
        gs[...] += dot_nn(lowt[q, :rank], gg[...])
        us[...] += dot_nn(lowt[q, rank:2 * rank], ug[...])

    events = arrival_order(hops, CHUNKS)
    left = {q: 2 * nz for q in range(CHUNKS)}
    waiting, todo, seen, done = [], [], 0, []
    plan = {
        0: [lambda: prepare(2)],
        1: [lambda: prepare(3), lows[0]],
        3: [lows[1]],
        5: [lows[2]],
        7: [lows[3]],
        8: [use_lows],
        11: [first_dp[1]],
    }
    last_step = 8 * (CHUNKS * hops) // 16
    scale = lambda k: k * (CHUNKS * hops) // 16
    steps = {}
    for k, fs in plan.items():
        steps.setdefault(scale(k), []).extend(fs)
    posted = 0
    ready = False

    def settle():
        found = []
        for slot, offset, q in waiting:
            wait_bytes(piece(offset, 1 - c, q), pair_recv.at[slot, q])
            found.append((block(offset, 1 - c), q))
        waiting.clear()
        return found

    started = False
    for hop, q in events:
        if hop == 0:
            fresh = pass_on(0, q)
            todo.append((t_me, q))
            waiting.extend(fresh)
            continue
        if not started:
            for copy in loads[1:]:
                copy.wait()
            prepare(0)
            prepare(1)
            wait_bytes(wv, w_sem)
            started = True
        items = [(block(offset, c), q) for _, offset in arrivals(hop)]
        for slot, offset in arrivals(hop):
            wait_bytes(piece(offset, c, q), ring_recv.at[slot, q])
        fresh = pass_on(hop, q)
        items = settle() + items + todo
        todo.clear()
        for f in steps.get(seen, []):
            f()
        held = [(b, p) for b, p in items if p >= 2 + seen]
        items = [(b, p) for b, p in items if p < 2 + seen]
        todo.extend(held)
        multiply(items)
        for _, p in items:
            left[p] -= 1
        waiting.extend(fresh)
        seen += 1
        while posted < CHUNKS and left[posted] == 0:
            post(posted)
            posted += 1
    items = settle() + todo
    multiply(items)
    while posted < CHUNKS:
        post(posted)
        posted += 1

    backs[0]()
    for r in range(4):
        at = slice(16 * r, 16 * r + 16)
        for k, full in ((0, gs), (2, us)):
            sb[4 * r + k] = (SCALE * full[at, :640]).astype(BF16)
            sb[4 * r + k + 1, :, :f_local - 640] = (SCALE * full[at, 640:]).astype(BF16)
    second_dp[0]()
    backs[1]()
    backs[2]()
    second_dp[1]()
    backs[3]()
    backs[4]()
    back_t = jnp.transpose(bk[...].astype(F32)).astype(BF16)
    firsts = SCALE * dot_nn(back_t, xin[...])
    for r in range(4):
        for k in range(2):
            for m in range(2):
                sc[4 * r + 2 * k + m] = firsts[
                    k * rank + 16 * r:k * rank + 16 * r + 16, 128 * m:128 * m + 128].astype(BF16)
    third_dp[0]()
    third_dp[1]()
    lows[5]()
    backs[5]()
    wait_bytes(cg.at[0:2 * hops - 1], ring_send)
    wait_bytes(cg.at[0:2 * hops], pair_send)
    first_dp[2]()
    second_dp[2]()
    third_dp[2]()


def unpack_kernel(a_ref, b_ref, c_ref, gf, gs, uf, us, gda, dsec):
    f_local = gs.shape[1]
    d_local = gf.shape[1]
    third = f_local // 3
    for r in range(4):
        at = slice(16 * r, 16 * r + 16)
        for k in range(3):
            gda[at, k * third:(k + 1) * third] = a_ref[4 * r + k].astype(F32)
        dsec[at] = a_ref[4 * r + 3, :, :d_local].astype(F32)
        for k, full in ((0, gs), (2, us)):
            full[at, :640] = b_ref[4 * r + k].astype(F32)
            full[at, 640:] = b_ref[4 * r + k + 1, :, :f_local - 640].astype(F32)
        for k, full in ((0, gf), (2, uf)):
            full[at, :128] = c_ref[4 * r + k].astype(F32)
            full[at, 128:] = c_ref[4 * r + k + 1].astype(F32)


def local(nz, nd, inputs, cotangent, gate_pre, up_pre, down_weight, gate_a, gate_b, up_a, up_b, down_a, down_second):
    tokens, d_local = inputs.shape
    f_local = gate_pre.shape[1]
    rank = gate_b.shape[0]
    nt, hops = 2 * nz, nz // 2
    rows, half = tokens // CHUNKS, tokens // 2
    part, group = half // nz, 16 // nd
    wide_a, wide_b, wide_c = f_local // 3, 640, 128
    any_space = pl.BlockSpec(memory_space=pl.ANY)
    vmem, dma = pltpu.VMEM, pltpu.SemaphoreType.DMA

    def dp_buffers(width):
        return [vmem((16, 16, width), BF16), vmem((nd - 1, group, 16, width), BF16), vmem((group, 16, width), BF16)]

    def z_buffers(width):
        return [vmem((tokens, width), F32), vmem((half, width), F32), vmem((nz, part, width), BF16),
                vmem((nz - 1, part, width), BF16), vmem((tokens, width), BF16)]

    scratch = [
        vmem((nt, tokens, d_local), BF16),
        vmem((nt, f_local, d_local), BF16),
        vmem((tokens, f_local), BF16),
        vmem((tokens, f_local), BF16),
        vmem((CHUNKS, rows, f_local), F32),
        vmem((CHUNKS, rows, f_local), F32),
        vmem((tokens, f_local), BF16),
        vmem((tokens, d_local), BF16),
        vmem((6 * rank, f_local), BF16),
        vmem((4 * rank, d_local), BF16),
        vmem((CHUNKS, rows, f_local), F32),
        *z_buffers(4 * rank),
        vmem((CHUNKS, 4 * rank, rows), BF16),
        *z_buffers(2 * rank),
        vmem((rank, f_local), F32),
        vmem((rank, f_local), F32),
        vmem((rank, f_local), F32),
        vmem((rank, d_local), F32),
        vmem((rows, f_local), BF16),
        vmem((rows, f_local), BF16),
        *dp_buffers(wide_a),
        *dp_buffers(wide_b),
        *dp_buffers(wide_c),
        dma((10,)),
        dma,
        dma((2 * hops - 1, CHUNKS)),
        dma((2 * hops, CHUNKS)),
        dma,
        dma,
        dma((16,)),
        dma((12,)),
        dma((3,)),
    ]
    packed = pl.pallas_call(
        functools.partial(main_kernel, nz, nd),
        out_shape=[jax.ShapeDtypeStruct((16, 16, w), BF16) for w in (wide_a, wide_b, wide_c)],
        in_specs=[any_space] * 11,
        out_specs=[any_space] * 3,
        scratch_shapes=scratch,
        compiler_params=pltpu.CompilerParams(
            collective_id=0, has_side_effects=True, vmem_limit_bytes=56 * 1024 * 1024),
        name="adapters",
    )(inputs, cotangent, gate_pre, up_pre, down_weight, gate_a.T, gate_b, up_a.T, up_b, down_a.T, down_second)
    small = jax.ShapeDtypeStruct((rank, d_local), F32)
    large = jax.ShapeDtypeStruct((rank, f_local), F32)
    gf, gs, uf, us, gda, dsec = pl.pallas_call(
        unpack_kernel, out_shape=[small, large, small, large, large, small], name="unpack")(*packed)
    return gf.T, gs, uf.T, us, gda.T, dsec


def solution(mesh):
    split, rows, columns = P("dp", "tensor"), P("tensor", None), P(None, "tensor")
    return jax.shard_map(
        functools.partial(local, mesh.shape["tensor"] // 2, mesh.shape["dp"]),
        mesh=mesh,
        in_specs=(split, split, split, split, rows, rows, columns, rows, columns, rows, columns),
        out_specs=(rows, columns, rows, columns, rows, columns),
        check_vma=False,
    )
```

```python
import functools

import jax
import jax.numpy as jnp
from jax import lax
from jax.experimental import pallas as pl
from jax.experimental.pallas import tpu as pltpu
from jax.sharding import PartitionSpec as P

MESH = pl.DeviceIdType.MESH
F32, BF16 = jnp.float32, jnp.bfloat16
CHUNKS = 3
PIECES = 2
DEPTH = 8
SCALE = 2.0
LOW_AT, LAG = (2, 9, 16, 22, 25, 33, 34), 2


def dot_nn(a, b):
    return jnp.dot(a, b, preferred_element_type=F32)


def dot_nt(a, b):
    return lax.dot_general(a, b, (((1,), (1,)), ((), ())), preferred_element_type=F32)


def travel_order(hops):
    own = [(0, b, q * PIECES + s) for q in range(CHUNKS) for b in range(2) for s in range(PIECES)]
    events, sent, at = [], [], 0

    def run(event):
        events.append(event)
        hop, b, s = event
        if hop + 1 < hops or (hop + 1 == hops and b == 0):
            sent.append((hop + 1, b, s))

    while own and len(sent) < DEPTH:
        run(own.pop(0))
    while at < len(sent):
        run(sent[at])
        at += 1
        while own and len(sent) - at < DEPTH:
            run(own.pop(0))
    return events


def main_kernel(
    nz, nd,
    x_hbm, c_hbm, g_hbm, u_hbm, w_hbm, ga_hbm, gb_hbm, ua_hbm, ub_hbm, da_hbm, ds_hbm,
    oa_hbm, ob_hbm, oc_hbm,
    cg, wv, gv, uv, act, usl, hid, xin, wf, wd, acc,
    lp, lpr, fsa, fra, tsa, tra, fsb, frb, tsb, trb, lowa, lowb, lowta, lowtb,
    bp, bpr, bsb, brb, esb, erb, bk,
    gs, us, gda, dsec, gg, ug,
    sa, ra, ta, sb, rb, tb, sc, rc, tc,
    in_sem, w_sem, ring_recv, pair_recv, ring_send, pair_send, red_sem, dp_sem, out_sem,
):
    tokens, d_local = x_hbm.shape
    f_local = g_hbm.shape[1]
    rank = gb_hbm.shape[0]
    nt = 2 * nz
    hops = nz // 2
    rows = tokens // CHUNKS
    half = tokens // 2
    part = half // nz
    group = 16 // nd
    early = (CHUNKS - 1) * rows
    short = rows // PIECES

    t_me = lax.axis_index("tensor")
    d_me = lax.axis_index("dp")
    z = t_me // 2
    c = t_me % 2
    way = 1 - 2 * c

    def at_z(offset):
        return lax.rem(z + offset + 2 * nz, nz)

    def block(offset, core):
        return 2 * at_z(offset) + core

    def remote(src, dst, send, recv, **where):
        return pltpu.make_async_remote_copy(
            src_ref=src, dst_ref=dst, send_sem=send, recv_sem=recv, device_id=where, device_id_type=MESH)

    def wait_bytes(ref, sem):
        pltpu.make_async_copy(ref, ref, sem).wait()

    loads = [
        pltpu.make_async_copy(c_hbm, cg.at[t_me], in_sem.at[0]),
        pltpu.make_async_copy(g_hbm, gv, in_sem.at[1]),
        pltpu.make_async_copy(u_hbm, uv, in_sem.at[2]),
        pltpu.make_async_copy(x_hbm, xin, in_sem.at[3]),
        pltpu.make_async_copy(ga_hbm, wd.at[0:rank], in_sem.at[4]),
        pltpu.make_async_copy(ua_hbm, wd.at[rank:2 * rank], in_sem.at[5]),
        pltpu.make_async_copy(ds_hbm, wd.at[3 * rank:4 * rank], in_sem.at[6]),
        pltpu.make_async_copy(gb_hbm, wf.at[0:rank], in_sem.at[7]),
        pltpu.make_async_copy(ub_hbm, wf.at[2 * rank:3 * rank], in_sem.at[8]),
        pltpu.make_async_copy(da_hbm, wf.at[4 * rank:5 * rank], in_sem.at[9]),
    ]
    for copy in loads:
        copy.start()
    w_loads = [
        pltpu.make_async_copy(w_hbm.at[:, k * d_local:(k + 1) * d_local], wv.at[k], w_sem) for k in range(nt)
    ]

    barrier = pltpu.get_barrier_semaphore()
    for k in range(1, nt):
        pl.semaphore_signal(barrier, inc=1, device_id={"tensor": lax.rem(t_me + k, nt)}, device_id_type=MESH)
    for k in range(1, nd):
        pl.semaphore_signal(barrier, inc=1, device_id={"dp": lax.rem(d_me + k, nd)}, device_id_type=MESH)

    zeros = jnp.zeros((rank, f_local), BF16)
    wf[rank:2 * rank] = zeros
    wf[3 * rank:4 * rank] = zeros
    wf[5 * rank:6 * rank] = zeros
    wd[2 * rank:3 * rank] = jnp.zeros((rank, d_local), BF16)
    for r in range(4):
        sa[4 * r + 3, :, d_local:] = jnp.zeros((16, sa.shape[2] - d_local), BF16)
        for k in (1, 3):
            sb[4 * r + k, :, f_local - 640:] = jnp.zeros((16, 1280 - f_local), BF16)
    gs[...] = jnp.zeros_like(gs)
    us[...] = jnp.zeros_like(us)

    loads[0].wait()
    pl.semaphore_wait(barrier, nt + nd - 2)

    def piece(offset, core, q):
        return cg.at[block(offset, core), q * short:(q + 1) * short]

    def core_of(b):
        return c if b == 0 else 1 - c

    def ring_on(hop, b, q):
        src = piece(-way * hop, core_of(b), q)
        remote(src, src, ring_send, ring_recv.at[2 * hop + b, q], tensor=block(way, c)).start()

    def pair_on(hop, b, q):
        src = piece(-way * hop, core_of(b), q)
        slot = 0 if hop == 0 else 2 * hop - 1 + b
        remote(src, src, pair_send, pair_recv.at[slot, q], tensor=2 * z + 1 - c).start()

    def ring_wait(hop, b, q):
        wait_bytes(piece(-way * hop, core_of(b), q), ring_recv.at[2 * (hop - 1) + b, q])

    def pair_wait(hop, b, q):
        slot = 0 if hop == 0 else 2 * hop - 1 + b
        wait_bytes(piece(way * hop, 1 - core_of(b), q), pair_recv.at[slot, q])

    def multiply(hop, q):
        if hop == 0:
            pair = [t_me, 2 * z + 1 - c]
        else:
            pair = [block(-way * hop, c), block(way * hop, 1 - c)]
            if hop < hops:
                pair += [block(-way * hop, 1 - c), block(way * hop, c)]
        at = slice(q * rows, (q + 1) * rows)
        total = dot_nt(cg[pair[0], at], wv[pair[0]])
        for b in pair[1:]:
            total += dot_nt(cg[b, at], wv[b])
        acc[q] = total if hop == 0 else acc[q] + total

    def prepare(q):
        def body(i, carry):
            at = pl.multiple_of(q * rows + i * 16, 16)
            g = gv[pl.ds(at, 16)].astype(F32)
            u = uv[pl.ds(at, 16)].astype(F32)
            s = 0.5 * jnp.tanh(0.5 * g) + 0.5
            a = g * s
            inner = pl.multiple_of(i * 16, 16)
            act[q, pl.ds(inner, 16)] = a
            usl[q, pl.ds(inner, 16)] = u * (s * (1.0 + (g - a)))
            hid[pl.ds(at, 16)] = (a * u).astype(BF16)
            return carry

        lax.fori_loop(0, rows // 16, body, 0)
        here = slice(q * rows, (q + 1) * rows)
        lp[here, :2 * rank] = dot_nt(xin[here], wd[:2 * rank])
        own = cg[t_me, q * rows:(q + 1) * rows]
        lp[here, 2 * rank:] = dot_nt(hid[here], wf[4 * rank:6 * rank]) + SCALE * dot_nt(own, wd[2 * rank:4 * rank])

    def z_steps(full, count, recv, parts, result, base):
        half = count // 2
        part = half // nz
        mine = pl.ds(pl.multiple_of(c * half, 16), half)
        other = pl.ds(pl.multiple_of((1 - c) * half, 16), half)
        slice_rows = pl.ds(pl.multiple_of(c * half + z * part, 16), part)

        def exchange():
            remote(full.at[other], recv, red_sem.at[base], red_sem.at[base + 1], tensor=2 * z + 1 - c).start()

        def scatter():
            wait_bytes(recv, red_sem.at[base + 1])
            recv[...] += full[mine]
            for n, (cols, out_b, in_b) in enumerate(parts):
                for k in range(nz):
                    out_b[k] = recv[k * part:(k + 1) * part, cols].astype(out_b.dtype)
                for k in range(1, nz):
                    to = at_z(k)
                    remote(out_b.at[to], in_b.at[k - 1], red_sem.at[base + 6 + 2 * n], red_sem.at[base + 7 + 2 * n],
                           tensor=2 * to + c).start()

        def gather():
            for n, (cols, out_b, in_b) in enumerate(parts):
                wait_bytes(in_b, red_sem.at[base + 7 + 2 * n])
                total = recv[pl.ds(pl.multiple_of(z * part, 16), part), cols]
                for k in range(nz - 1):
                    total += in_b[k].astype(F32)
                result[slice_rows, cols] = total.astype(BF16)
            for k in range(1, nz):
                remote(result.at[slice_rows], result.at[slice_rows], red_sem.at[base + 2], red_sem.at[base + 3],
                       tensor=block(k, c)).start()

        def share():
            wait_bytes(result.at[0:(nz - 1) * part], red_sem.at[base + 3])
            remote(result.at[mine], result.at[mine], red_sem.at[base + 4], red_sem.at[base + 5],
                   tensor=2 * z + 1 - c).start()

        def finish():
            wait_bytes(result.at[0:half], red_sem.at[base + 5])

        def drain():
            wait_bytes(recv, red_sem.at[base])
            for n, (cols, out_b, in_b) in enumerate(parts):
                wait_bytes(in_b, red_sem.at[base + 6 + 2 * n])
            wait_bytes(result.at[0:(nz - 1) * part], red_sem.at[base + 2])
            wait_bytes(result.at[0:half], red_sem.at[base + 4])

        return exchange, scatter, gather, share, finish, drain

    low_mine = pl.ds(pl.multiple_of(c * half, 16), half)
    low_other = pl.ds(pl.multiple_of((1 - c) * half, 16), half)
    low_rows = pl.ds(pl.multiple_of(c * half + z * part, 16), part)
    low_parts = [(slice(0, 2 * rank), fsa, fra, tsa, tra), (slice(2 * rank, 4 * rank), fsb, frb, tsb, trb)]

    def low_part(offset, cols):
        return lpr[pl.ds(pl.multiple_of(at_z(offset) * part, 16), part), cols]

    def low_exchange():
        remote(lp.at[low_other], lpr, red_sem.at[0], red_sem.at[1], tensor=2 * z + 1 - c).start()

    def low_near():
        wait_bytes(lpr, red_sem.at[1])
        lpr[...] += lp[low_mine]
        for n, (cols, near_out, near_in, _, _) in enumerate(low_parts):
            for k, offset in enumerate((4 * way, way, -2 * way, -way, 2 * way)):
                near_out[k] = low_part(offset, cols).astype(near_out.dtype)
            for step, some in ((way, slice(0, 3)), (-way, slice(3, 5))):
                remote(near_out.at[some], near_in.at[some], red_sem.at[2 + n], red_sem.at[4 + n],
                       tensor=block(step, c)).start()

    def low_far():
        for n, (cols, _, near_in, far_out, far_in) in enumerate(low_parts):
            wait_bytes(near_in, red_sem.at[4 + n])
            up = low_part(3 * way, cols) + near_in[0].astype(F32) + near_in[4].astype(F32)
            down = low_part(-3 * way, cols) + near_in[2].astype(F32)
            far_out[0] = up.astype(far_out.dtype)
            far_out[1] = down.astype(far_out.dtype)
            for k, step in ((0, 3 * way), (1, -3 * way)):
                remote(far_out.at[k], far_in.at[k], red_sem.at[6 + n], red_sem.at[8 + n], tensor=block(step, c)).start()

    def low_spread(result, base):
        for k in range(1, nz):
            remote(result.at[low_rows], result.at[low_rows], red_sem.at[base], red_sem.at[base + 1],
                   tensor=block(k, c)).start()

    def low_share(result, base):
        wait_bytes(result.at[0:(nz - 1) * part], red_sem.at[base + 1])
        remote(result.at[low_mine], result.at[low_mine], red_sem.at[base + 2], red_sem.at[base + 3],
               tensor=2 * z + 1 - c).start()

    def low_sum():
        for n, (cols, _, near_in, _, far_in) in enumerate(low_parts):
            wait_bytes(far_in, red_sem.at[8 + n])
            total = low_part(0, cols) + near_in[1].astype(F32) + near_in[3].astype(F32)
            total += far_in[0].astype(F32) + far_in[1].astype(F32)
            (lowa, lowb)[n][low_rows] = total.astype(BF16)
        low_spread(lowb, 32)

    def low_drain():
        wait_bytes(lpr, red_sem.at[0])
        for n, (_, _, near_in, _, far_in) in enumerate(low_parts):
            wait_bytes(near_in, red_sem.at[2 + n])
            wait_bytes(far_in, red_sem.at[6 + n])
        for result, base in ((lowa, 28), (lowb, 32)):
            wait_bytes(result.at[0:(nz - 1) * part], red_sem.at[base])
            wait_bytes(result.at[0:half], red_sem.at[base + 2])

    def last_scatter():
        share = rows // nt
        for k in range(nt):
            esb[k] = bp[early + k * share:early + (k + 1) * share].astype(BF16)
        for k in range(1, nt):
            to = lax.rem(t_me + k, nt)
            remote(esb.at[to], erb.at[k - 1], red_sem.at[20], red_sem.at[21], tensor=to).start()

    def last_gather():
        share = rows // nt
        mine = pl.ds(pl.multiple_of(early + t_me * share, 16), share)
        wait_bytes(erb, red_sem.at[21])
        total = bp[mine]
        for k in range(nt - 1):
            total += erb[k].astype(F32)
        bk[mine] = total.astype(BF16)
        for k in range(1, nt):
            remote(bk.at[mine], bk.at[mine], red_sem.at[22], red_sem.at[23], tensor=lax.rem(t_me + k, nt)).start()

    def last_finish():
        wait_bytes(bk.at[0:rows - rows // nt], red_sem.at[23])

    def last_drain():
        wait_bytes(erb, red_sem.at[20])
        wait_bytes(bk.at[0:rows - rows // nt], red_sem.at[22])

    def dp_steps(out_b, in_b, total_b, result, base):
        def scatter():
            for k in range(1, nd):
                to = lax.rem(d_me + k, nd)
                remote(out_b.at[pl.ds(to * group, group)], in_b.at[k - 1], dp_sem.at[base], dp_sem.at[base + 1],
                       dp=to).start()

        def gather():
            wait_bytes(in_b, dp_sem.at[base + 1])
            total = out_b[pl.ds(d_me * group, group)].astype(F32)
            for k in range(nd - 1):
                total += in_b[k].astype(F32)
            total_b[...] = total.astype(BF16)
            place = result.at[pl.ds(d_me * group, group)]
            for k in range(1, nd):
                remote(total_b, place, dp_sem.at[base + 2], dp_sem.at[base + 3], dp=lax.rem(d_me + k, nd)).start()
            pltpu.make_async_copy(total_b, place, out_sem.at[base // 4]).start()

        def finish():
            place = result.at[pl.ds(d_me * group, group)]
            pltpu.make_async_copy(total_b, place, out_sem.at[base // 4]).wait()
            wait_bytes(result.at[0:(nd - 1) * group], dp_sem.at[base + 3])
            wait_bytes(in_b, dp_sem.at[base])
            wait_bytes(result.at[0:(nd - 1) * group], dp_sem.at[base + 2])

        return scatter, gather, finish

    backs = z_steps(bp, early, bpr, [(slice(0, 2 * rank), bsb, brb)], bk, 10)
    first_dp = dp_steps(sa, ra, ta, oa_hbm, 0)
    second_dp = dp_steps(sb, rb, tb, ob_hbm, 4)
    third_dp = dp_steps(sc, rc, tc, oc_hbm, 8)

    def use_lows():
        wait_bytes(lowb.at[0:half], red_sem.at[35])
        for q in range(CHUNKS):
            lowtb[q] = jnp.transpose(lowb[q * rows:(q + 1) * rows].astype(F32)).astype(BF16)
        gda[...] = jnp.zeros_like(gda)
        dsec[...] = jnp.zeros_like(dsec)

        def body(q, carry):
            at = pl.ds(pl.multiple_of(q * rows, 16), rows)
            gda[...] += dot_nn(lowtb[q, rank:], hid[at])
            dsec[...] += dot_nn(lowtb[q, :rank], cg[t_me, at])
            return carry

        lax.fori_loop(0, CHUNKS, body, 0)
        third = f_local // 3
        for r in range(4):
            at = slice(16 * r, 16 * r + 16)
            for k in range(3):
                sa[4 * r + k] = gda[at, k * third:(k + 1) * third].astype(BF16)
            sa[4 * r + 3, :, :d_local] = (SCALE * dsec[at]).astype(BF16)
        first_dp[0]()

    def second_gradients():
        low_share(lowa, 28)
        wait_bytes(lowa.at[0:half], red_sem.at[31])
        for q in range(CHUNKS):
            lowta[q] = jnp.transpose(lowa[q * rows:(q + 1) * rows].astype(F32)).astype(BF16)

        def body(q, carry):
            at = pl.ds(pl.multiple_of(q * rows, 16), rows)
            gs[...] += dot_nn(lowta[q, :rank], gg[at])
            us[...] += dot_nn(lowta[q, rank:], ug[at])
            return carry

        lax.fori_loop(0, CHUNKS, body, 0)

    def post(q):
        here = slice(q * rows, (q + 1) * rows)
        lowq = lowb[here]
        width = f_local // 3

        def body(i, carry):
            cols = pl.ds(pl.multiple_of(i * width, 128), width)
            grad = acc[q, :, cols] + dot_nn(lowq, wf[3 * rank:5 * rank, cols])
            gg[here, cols] = (grad * usl[q, :, cols]).astype(BF16)
            ug[here, cols] = (grad * act[q, :, cols]).astype(BF16)
            return carry

        lax.fori_loop(0, 3, body, 0)
        bp[here] = dot_nt(gg[here], wf[:2 * rank]) + dot_nt(ug[here], wf[rank:3 * rank])
        if q == CHUNKS - 2:
            backs[0]()
        if q == CHUNKS - 1:
            last_scatter()

    events = travel_order(hops)
    arrivals = [e for e in events if e[0] > 0]
    count = len(arrivals)
    def take(hop, q):
        for s in range(q * PIECES, (q + 1) * PIECES):
            for b in range(2 if 0 < hop < hops else 1 if hop else 0):
                pair_wait(hop, b, s)
        multiply(hop, q)

    def last_own():
        wait_bytes(wv, w_sem)

    tasks = [(1, last_own)]
    tasks += list(zip(LOW_AT, [
        low_near, low_far, low_sum, lambda: low_share(lowb, 32), use_lows, first_dp[1], lambda: low_spread(lowa, 28)]))
    done = 0
    finished = {}
    for e in events:
        hop, b, s = e
        done += hop > 0
        finished[hop, s // PIECES] = done
    lows_at = LOW_AT[4]
    for (hop, q), at in finished.items():
        ready = at + 1 if hop == 0 else at + LAG
        tasks.append((ready, functools.partial(take, hop, q)))
        if hop == hops:
            ready = max(finished[h, q] for h in range(hops + 1)) + LAG
            at = max(ready, lows_at) + 1 + q if q < CHUNKS - 1 else max(ready, lows_at + CHUNKS, count) + 1
            tasks.append((at, functools.partial(post, q)))
            if q == CHUNKS - 2:
                tasks += [(at + 3, backs[1]), (at + 9, backs[2])]
    tasks.sort(key=lambda t: t[0])

    for q in range(CHUNKS * PIECES):
        pair_on(0, 0, q)
    done, first = 0, True
    for hop, b, s in events:
        if hop == 0:
            if b == 1:
                pair_wait(0, 0, s)
            ring_on(0, b, s)
            continue
        if first:
            for copy in loads[1:]:
                copy.wait()
            for copy in w_loads:
                copy.start()
            for n in range(CHUNKS):
                prepare(n)
            low_exchange()
            first = False
        ring_wait(hop, b, s)
        if hop + 1 < hops or (hop + 1 == hops and b == 0):
            ring_on(hop, b, s)
        pair_on(hop, b, s)
        done += 1
        if tasks and tasks[0][0] <= done:
            tasks.pop(0)[1]()
    while tasks:
        tasks.pop(0)[1]()

    second_gradients()
    for r in range(4):
        at = slice(16 * r, 16 * r + 16)
        for k, full in ((0, gs), (2, us)):
            sb[4 * r + k] = (SCALE * full[at, :640]).astype(BF16)
            sb[4 * r + k + 1, :, :f_local - 640] = (SCALE * full[at, 640:]).astype(BF16)
    second_dp[0]()
    last_gather()
    backs[3]()
    backs[4]()
    back_t = jnp.transpose(bk[:early].astype(F32)).astype(BF16)
    firsts = dot_nn(back_t, xin[:early])
    last_finish()
    back_t = jnp.transpose(bk[early:].astype(F32)).astype(BF16)
    firsts = SCALE * (firsts + dot_nn(back_t, xin[early:]))
    for r in range(4):
        for k in range(2):
            for m in range(2):
                sc[4 * r + 2 * k + m] = firsts[
                    k * rank + 16 * r:k * rank + 16 * r + 16, 128 * m:128 * m + 128].astype(BF16)
    third_dp[0]()
    second_dp[1]()
    low_drain()
    backs[5]()
    last_drain()
    wait_bytes(cg.at[0:2 * hops - 1], ring_send)
    wait_bytes(cg.at[0:2 * hops], pair_send)
    third_dp[1]()
    first_dp[2]()
    second_dp[2]()
    third_dp[2]()


def unpack_kernel(a_ref, b_ref, c_ref, gf, gs, uf, us, gda, dsec):
    f_local = gs.shape[1]
    d_local = gf.shape[1]
    third = f_local // 3
    for r in range(4):
        at = slice(16 * r, 16 * r + 16)
        for k in range(3):
            gda[at, k * third:(k + 1) * third] = a_ref[4 * r + k].astype(F32)
        dsec[at] = a_ref[4 * r + 3, :, :d_local].astype(F32)
        for k, full in ((0, gs), (2, us)):
            full[at, :640] = b_ref[4 * r + k].astype(F32)
            full[at, 640:] = b_ref[4 * r + k + 1, :, :f_local - 640].astype(F32)
        for k, full in ((0, gf), (2, uf)):
            full[at, :128] = c_ref[4 * r + k].astype(F32)
            full[at, 128:] = c_ref[4 * r + k + 1].astype(F32)


def local(nz, nd, inputs, cotangent, gate_pre, up_pre, down_weight, gate_a, gate_b, up_a, up_b, down_a, down_second):
    tokens, d_local = inputs.shape
    f_local = gate_pre.shape[1]
    rank = gate_b.shape[0]
    nt, hops = 2 * nz, nz // 2
    rows, half = tokens // CHUNKS, tokens // 2
    part, group = half // nz, 16 // nd
    wide_a, wide_b, wide_c = f_local // 3, 640, 128
    any_space = pl.BlockSpec(memory_space=pl.ANY)
    vmem, dma = pltpu.VMEM, pltpu.SemaphoreType.DMA

    def dp_buffers(width):
        return [vmem((16, 16, width), BF16), vmem((nd - 1, group, 16, width), BF16), vmem((group, 16, width), BF16)]

    early, wide_low, wide_back = tokens - rows, 4 * rank, 2 * rank
    spread = early // nt

    scratch = [
        vmem((nt, tokens, d_local), BF16),
        vmem((nt, f_local, d_local), BF16),
        vmem((tokens, f_local), BF16),
        vmem((tokens, f_local), BF16),
        vmem((CHUNKS, rows, f_local), F32),
        vmem((CHUNKS, rows, f_local), F32),
        vmem((tokens, f_local), BF16),
        vmem((tokens, d_local), BF16),
        vmem((6 * rank, f_local), BF16),
        vmem((4 * rank, d_local), BF16),
        vmem((CHUNKS, rows, f_local), F32),
        vmem((tokens, wide_low), F32),
        vmem((half, wide_low), F32),
        vmem((5, part, wide_back), BF16),
        vmem((5, part, wide_back), BF16),
        vmem((2, part, wide_back), BF16),
        vmem((2, part, wide_back), BF16),
        vmem((5, part, wide_back), F32),
        vmem((5, part, wide_back), F32),
        vmem((2, part, wide_back), F32),
        vmem((2, part, wide_back), F32),
        vmem((tokens, wide_back), BF16),
        vmem((tokens, wide_back), BF16),
        vmem((CHUNKS, wide_back, rows), BF16),
        vmem((CHUNKS, wide_back, rows), BF16),
        vmem((tokens, wide_back), F32),
        vmem((early // 2, wide_back), F32),
        vmem((nz, spread, wide_back), BF16),
        vmem((nz - 1, spread, wide_back), BF16),
        vmem((nt, rows // nt, wide_back), BF16),
        vmem((nt - 1, rows // nt, wide_back), BF16),
        vmem((tokens, wide_back), BF16),
        vmem((rank, f_local), F32),
        vmem((rank, f_local), F32),
        vmem((rank, f_local), F32),
        vmem((rank, d_local), F32),
        vmem((tokens, f_local), BF16),
        vmem((tokens, f_local), BF16),
        *dp_buffers(wide_a),
        *dp_buffers(wide_b),
        *dp_buffers(wide_c),
        dma((10,)),
        dma,
        dma((2 * hops - 1, CHUNKS * PIECES)),
        dma((2 * hops, CHUNKS * PIECES)),
        dma,
        dma,
        dma((36,)),
        dma((12,)),
        dma((3,)),
    ]
    packed = pl.pallas_call(
        functools.partial(main_kernel, nz, nd),
        out_shape=[jax.ShapeDtypeStruct((16, 16, w), BF16) for w in (wide_a, wide_b, wide_c)],
        in_specs=[any_space] * 11,
        out_specs=[any_space] * 3,
        scratch_shapes=scratch,
        compiler_params=pltpu.CompilerParams(
            collective_id=0, has_side_effects=True, vmem_limit_bytes=56 * 1024 * 1024),
        name="adapters",
    )(inputs, cotangent, gate_pre, up_pre, down_weight, gate_a.T, gate_b, up_a.T, up_b, down_a.T, down_second)
    small = jax.ShapeDtypeStruct((rank, d_local), F32)
    large = jax.ShapeDtypeStruct((rank, f_local), F32)
    gf, gs, uf, us, gda, dsec = pl.pallas_call(
        unpack_kernel, out_shape=[small, large, small, large, large, small], name="unpack")(*packed)
    return gf.T, gs, uf.T, us, gda.T, dsec


def solution(mesh):
    split, rows, columns = P("dp", "tensor"), P("tensor", None), P(None, "tensor")
    return jax.shard_map(
        functools.partial(local, mesh.shape["tensor"] // 2, mesh.shape["dp"]),
        mesh=mesh,
        in_specs=(split, split, split, split, rows, rows, columns, rows, columns, rows, columns),
        out_specs=(rows, columns, rows, columns, rows, columns),
        check_vma=False,
    )
```

```python
import functools

import jax
import jax.numpy as jnp
from jax import lax
from jax.experimental import pallas as pl
from jax.experimental.pallas import tpu as pltpu
from jax.sharding import PartitionSpec as P

MESH = pl.DeviceIdType.MESH
F32, BF16 = jnp.float32, jnp.bfloat16
CHUNKS = 3
PIECES = 2
DEPTH = 8
SCALE = 2.0
LOW_AT, LAG = (2, 13, 24, 34, 37, 41, 38), 2


def dot_nn(a, b):
    return jnp.dot(a, b, preferred_element_type=F32)


def dot_nt(a, b):
    return lax.dot_general(a, b, (((1,), (1,)), ((), ())), preferred_element_type=F32)


def travel_order(hops):
    own = [(0, b, q * PIECES + s) for q in range(CHUNKS) for b in range(2) for s in range(PIECES)]
    events, sent, at = [], [], 0

    def run(event):
        events.append(event)
        hop, b, s = event
        if hop + 1 < hops or (hop + 1 == hops and b == 0):
            sent.append((hop + 1, b, s))

    while own and len(sent) < DEPTH:
        run(own.pop(0))
    while at < len(sent):
        run(sent[at])
        at += 1
        while own and len(sent) - at < DEPTH:
            run(own.pop(0))
    return events


def main_kernel(
    nz, nd,
    x_hbm, c_hbm, g_hbm, u_hbm, w_hbm, ga_hbm, gb_hbm, ua_hbm, ub_hbm, da_hbm, ds_hbm,
    oa_hbm, ob_hbm, oc_hbm,
    cg, wv, gv, uv, act, usl, hid, xin, wf, wd, acc,
    lp, lpr, fsa, fra, tsa, tra, fsb, frb, tsb, trb, lowa, lowb, lowta, lowtb,
    bp, bpr, bsb, brb, esb, erb, bk,
    gs, us, gda, dsec, gg, ug,
    sa, ra, ta, sb, rb, tb, sc, rc, tc,
    in_sem, w_sem, ring_recv, pair_recv, ring_send, pair_send, red_sem, dp_sem, out_sem,
):
    tokens, d_local = x_hbm.shape
    f_local = g_hbm.shape[1]
    rank = gb_hbm.shape[0]
    nt = 2 * nz
    hops = nz // 2
    rows = tokens // CHUNKS
    half = tokens // 2
    part = half // nz
    group = 16 // nd
    early = (CHUNKS - 1) * rows
    short = rows // PIECES

    t_me = lax.axis_index("tensor")
    d_me = lax.axis_index("dp")
    z = t_me // 2
    c = t_me % 2
    way = 1 - 2 * c

    def at_z(offset):
        return lax.rem(z + offset + 2 * nz, nz)

    def block(offset, core):
        return 2 * at_z(offset) + core

    def remote(src, dst, send, recv, **where):
        return pltpu.make_async_remote_copy(
            src_ref=src, dst_ref=dst, send_sem=send, recv_sem=recv, device_id=where, device_id_type=MESH)

    def wait_bytes(ref, sem):
        pltpu.make_async_copy(ref, ref, sem).wait()

    loads = [
        pltpu.make_async_copy(c_hbm, cg.at[t_me], in_sem.at[0]),
        pltpu.make_async_copy(g_hbm, gv, in_sem.at[1]),
        pltpu.make_async_copy(u_hbm, uv, in_sem.at[2]),
        pltpu.make_async_copy(x_hbm, xin, in_sem.at[3]),
        pltpu.make_async_copy(ga_hbm, wd.at[0:rank], in_sem.at[4]),
        pltpu.make_async_copy(ua_hbm, wd.at[rank:2 * rank], in_sem.at[5]),
        pltpu.make_async_copy(ds_hbm, wd.at[3 * rank:4 * rank], in_sem.at[6]),
        pltpu.make_async_copy(gb_hbm, wf.at[0:rank], in_sem.at[7]),
        pltpu.make_async_copy(ub_hbm, wf.at[2 * rank:3 * rank], in_sem.at[8]),
        pltpu.make_async_copy(da_hbm, wf.at[4 * rank:5 * rank], in_sem.at[9]),
    ]
    for copy in loads:
        copy.start()
    w_loads = [
        pltpu.make_async_copy(w_hbm.at[:, k * d_local:(k + 1) * d_local], wv.at[k], w_sem) for k in range(nt)
    ]

    barrier = pltpu.get_barrier_semaphore()
    for k in range(1, nt):
        pl.semaphore_signal(barrier, inc=1, device_id={"tensor": lax.rem(t_me + k, nt)}, device_id_type=MESH)
    for k in range(1, nd):
        pl.semaphore_signal(barrier, inc=1, device_id={"dp": lax.rem(d_me + k, nd)}, device_id_type=MESH)

    zeros = jnp.zeros((rank, f_local), BF16)
    wf[rank:2 * rank] = zeros
    wf[3 * rank:4 * rank] = zeros
    wf[5 * rank:6 * rank] = zeros
    wd[2 * rank:3 * rank] = jnp.zeros((rank, d_local), BF16)
    for r in range(4):
        sa[4 * r + 3, :, d_local:] = jnp.zeros((16, sa.shape[2] - d_local), BF16)
        for k in (1, 3):
            sb[4 * r + k, :, f_local - 640:] = jnp.zeros((16, 1280 - f_local), BF16)
    gs[...] = jnp.zeros_like(gs)
    us[...] = jnp.zeros_like(us)

    loads[0].wait()
    pl.semaphore_wait(barrier, nt + nd - 2)

    def piece(offset, core, q):
        return cg.at[block(offset, core), q * short:(q + 1) * short]

    def core_of(b):
        return c if b == 0 else 1 - c

    def ring_on(hop, b, q):
        src = piece(-way * hop, core_of(b), q)
        remote(src, src, ring_send, ring_recv.at[2 * hop + b, q], tensor=block(way, c)).start()

    def pair_on(hop, b, q):
        src = piece(-way * hop, core_of(b), q)
        slot = 0 if hop == 0 else 2 * hop - 1 + b
        remote(src, src, pair_send, pair_recv.at[slot, q], tensor=2 * z + 1 - c).start()

    def ring_wait(hop, b, q):
        wait_bytes(piece(-way * hop, core_of(b), q), ring_recv.at[2 * (hop - 1) + b, q])

    def pair_wait(hop, b, q):
        slot = 0 if hop == 0 else 2 * hop - 1 + b
        wait_bytes(piece(way * hop, 1 - core_of(b), q), pair_recv.at[slot, q])

    def multiply(hop, q):
        if hop == 0:
            pair = [t_me, 2 * z + 1 - c]
        else:
            pair = [block(-way * hop, c), block(way * hop, 1 - c)]
            if hop < hops:
                pair += [block(-way * hop, 1 - c), block(way * hop, c)]
        at = slice(q * rows, (q + 1) * rows)
        total = dot_nt(cg[pair[0], at], wv[pair[0]])
        for b in pair[1:]:
            total += dot_nt(cg[b, at], wv[b])
        acc[q] = total if hop == 0 else acc[q] + total

    def prepare(q):
        def body(i, carry):
            at = pl.multiple_of(q * rows + i * 16, 16)
            g = gv[pl.ds(at, 16)].astype(F32)
            u = uv[pl.ds(at, 16)].astype(F32)
            s = 0.5 * jnp.tanh(0.5 * g) + 0.5
            a = g * s
            inner = pl.multiple_of(i * 16, 16)
            act[q, pl.ds(inner, 16)] = a
            usl[q, pl.ds(inner, 16)] = u * (s * (1.0 + (g - a)))
            hid[pl.ds(at, 16)] = (a * u).astype(BF16)
            return carry

        lax.fori_loop(0, rows // 16, body, 0)
        here = slice(q * rows, (q + 1) * rows)
        lp[here, :2 * rank] = dot_nt(xin[here], wd[:2 * rank])
        own = cg[t_me, q * rows:(q + 1) * rows]
        lp[here, 2 * rank:] = dot_nt(hid[here], wf[4 * rank:6 * rank]) + SCALE * dot_nt(own, wd[2 * rank:4 * rank])

    def z_steps(full, count, recv, parts, result, base):
        half = count // 2
        part = half // nz
        mine = pl.ds(pl.multiple_of(c * half, 16), half)
        other = pl.ds(pl.multiple_of((1 - c) * half, 16), half)
        slice_rows = pl.ds(pl.multiple_of(c * half + z * part, 16), part)

        def exchange():
            remote(full.at[other], recv, red_sem.at[base], red_sem.at[base + 1], tensor=2 * z + 1 - c).start()

        def scatter():
            wait_bytes(recv, red_sem.at[base + 1])
            recv[...] += full[mine]
            for n, (cols, out_b, in_b) in enumerate(parts):
                for k in range(nz):
                    out_b[k] = recv[k * part:(k + 1) * part, cols].astype(out_b.dtype)
                for k in range(1, nz):
                    to = at_z(k)
                    remote(out_b.at[to], in_b.at[k - 1], red_sem.at[base + 6 + 2 * n], red_sem.at[base + 7 + 2 * n],
                           tensor=2 * to + c).start()

        def gather():
            for n, (cols, out_b, in_b) in enumerate(parts):
                wait_bytes(in_b, red_sem.at[base + 7 + 2 * n])
                total = recv[pl.ds(pl.multiple_of(z * part, 16), part), cols]
                for k in range(nz - 1):
                    total += in_b[k].astype(F32)
                result[slice_rows, cols] = total.astype(BF16)
            for k in range(1, nz):
                remote(result.at[slice_rows], result.at[slice_rows], red_sem.at[base + 2], red_sem.at[base + 3],
                       tensor=block(k, c)).start()

        def share():
            wait_bytes(result.at[0:(nz - 1) * part], red_sem.at[base + 3])
            remote(result.at[mine], result.at[mine], red_sem.at[base + 4], red_sem.at[base + 5],
                   tensor=2 * z + 1 - c).start()

        def finish():
            wait_bytes(result.at[0:half], red_sem.at[base + 5])

        def drain():
            wait_bytes(recv, red_sem.at[base])
            for n, (cols, out_b, in_b) in enumerate(parts):
                wait_bytes(in_b, red_sem.at[base + 6 + 2 * n])
            wait_bytes(result.at[0:(nz - 1) * part], red_sem.at[base + 2])
            wait_bytes(result.at[0:half], red_sem.at[base + 4])

        return exchange, scatter, gather, share, finish, drain

    low_mine = pl.ds(pl.multiple_of(c * half, 16), half)
    low_other = pl.ds(pl.multiple_of((1 - c) * half, 16), half)
    low_rows = pl.ds(pl.multiple_of(c * half + z * part, 16), part)
    low_parts = [(slice(0, 2 * rank), fsa, fra, tsa, tra), (slice(2 * rank, 4 * rank), fsb, frb, tsb, trb)]

    def low_part(offset, cols):
        return lpr[pl.ds(pl.multiple_of(at_z(offset) * part, 16), part), cols]

    def low_exchange():
        remote(lp.at[low_other], lpr, red_sem.at[0], red_sem.at[1], tensor=2 * z + 1 - c).start()

    def low_near():
        wait_bytes(lpr, red_sem.at[1])
        lpr[...] += lp[low_mine]
        for n, (cols, near_out, near_in, _, _) in enumerate(low_parts):
            for k, offset in enumerate((4 * way, way, -2 * way, -way, 2 * way)):
                near_out[k] = low_part(offset, cols).astype(near_out.dtype)
            for step, some in ((way, slice(0, 3)), (-way, slice(3, 5))):
                remote(near_out.at[some], near_in.at[some], red_sem.at[2 + n], red_sem.at[4 + n],
                       tensor=block(step, c)).start()

    def low_far():
        for n, (cols, _, near_in, far_out, far_in) in enumerate(low_parts):
            wait_bytes(near_in, red_sem.at[4 + n])
            up = low_part(3 * way, cols) + near_in[0].astype(F32) + near_in[4].astype(F32)
            down = low_part(-3 * way, cols) + near_in[2].astype(F32)
            far_out[0] = up.astype(far_out.dtype)
            far_out[1] = down.astype(far_out.dtype)
            for k, step in ((0, 3 * way), (1, -3 * way)):
                remote(far_out.at[k], far_in.at[k], red_sem.at[6 + n], red_sem.at[8 + n], tensor=block(step, c)).start()

    def low_spread(result, base):
        for k in range(1, nz):
            remote(result.at[low_rows], result.at[low_rows], red_sem.at[base], red_sem.at[base + 1],
                   tensor=block(k, c)).start()

    def low_share(result, base):
        wait_bytes(result.at[0:(nz - 1) * part], red_sem.at[base + 1])
        remote(result.at[low_mine], result.at[low_mine], red_sem.at[base + 2], red_sem.at[base + 3],
               tensor=2 * z + 1 - c).start()

    def low_sum():
        for n, (cols, _, near_in, _, far_in) in enumerate(low_parts):
            wait_bytes(far_in, red_sem.at[8 + n])
            total = low_part(0, cols) + near_in[1].astype(F32) + near_in[3].astype(F32)
            total += far_in[0].astype(F32) + far_in[1].astype(F32)
            (lowa, lowb)[n][low_rows] = total.astype(BF16)
        low_spread(lowb, 32)

    def low_drain():
        wait_bytes(lpr, red_sem.at[0])
        for n, (_, _, near_in, _, far_in) in enumerate(low_parts):
            wait_bytes(near_in, red_sem.at[2 + n])
            wait_bytes(far_in, red_sem.at[6 + n])
        for result, base in ((lowa, 28), (lowb, 32)):
            wait_bytes(result.at[0:(nz - 1) * part], red_sem.at[base])
            wait_bytes(result.at[0:half], red_sem.at[base + 2])

    def last_scatter():
        share = rows // nt
        for k in range(nt):
            esb[k] = bp[early + k * share:early + (k + 1) * share].astype(BF16)
        for k in range(1, nt):
            to = lax.rem(t_me + k, nt)
            remote(esb.at[to], erb.at[k - 1], red_sem.at[20], red_sem.at[21], tensor=to).start()

    def last_gather():
        share = rows // nt
        mine = pl.ds(pl.multiple_of(early + t_me * share, 16), share)
        wait_bytes(erb, red_sem.at[21])
        total = bp[mine]
        for k in range(nt - 1):
            total += erb[k].astype(F32)
        bk[mine] = total.astype(BF16)
        for k in range(1, nt):
            remote(bk.at[mine], bk.at[mine], red_sem.at[22], red_sem.at[23], tensor=lax.rem(t_me + k, nt)).start()

    def last_finish():
        wait_bytes(bk.at[0:rows - rows // nt], red_sem.at[23])

    def last_drain():
        wait_bytes(erb, red_sem.at[20])
        wait_bytes(bk.at[0:rows - rows // nt], red_sem.at[22])

    def dp_steps(out_b, in_b, total_b, result, base):
        def scatter():
            for k in range(1, nd):
                to = lax.rem(d_me + k, nd)
                remote(out_b.at[pl.ds(to * group, group)], in_b.at[k - 1], dp_sem.at[base], dp_sem.at[base + 1],
                       dp=to).start()

        def gather():
            wait_bytes(in_b, dp_sem.at[base + 1])
            total = out_b[pl.ds(d_me * group, group)].astype(F32)
            for k in range(nd - 1):
                total += in_b[k].astype(F32)
            total_b[...] = total.astype(BF16)
            place = result.at[pl.ds(d_me * group, group)]
            for k in range(1, nd):
                remote(total_b, place, dp_sem.at[base + 2], dp_sem.at[base + 3], dp=lax.rem(d_me + k, nd)).start()
            pltpu.make_async_copy(total_b, place, out_sem.at[base // 4]).start()

        def finish():
            place = result.at[pl.ds(d_me * group, group)]
            pltpu.make_async_copy(total_b, place, out_sem.at[base // 4]).wait()
            wait_bytes(result.at[0:(nd - 1) * group], dp_sem.at[base + 3])
            wait_bytes(in_b, dp_sem.at[base])
            wait_bytes(result.at[0:(nd - 1) * group], dp_sem.at[base + 2])

        return scatter, gather, finish

    backs = z_steps(bp, early, bpr, [(slice(0, 2 * rank), bsb, brb)], bk, 10)
    first_dp = dp_steps(sa, ra, ta, oa_hbm, 0)
    second_dp = dp_steps(sb, rb, tb, ob_hbm, 4)
    third_dp = dp_steps(sc, rc, tc, oc_hbm, 8)

    def use_lows():
        wait_bytes(lowb.at[0:half], red_sem.at[35])
        for q in range(CHUNKS):
            lowtb[q] = jnp.transpose(lowb[q * rows:(q + 1) * rows].astype(F32)).astype(BF16)
        gda[...] = jnp.zeros_like(gda)
        dsec[...] = jnp.zeros_like(dsec)

        def body(q, carry):
            at = pl.ds(pl.multiple_of(q * rows, 16), rows)
            gda[...] += dot_nn(lowtb[q, rank:], hid[at])
            dsec[...] += dot_nn(lowtb[q, :rank], cg[t_me, at])
            return carry

        lax.fori_loop(0, CHUNKS, body, 0)
        third = f_local // 3
        for r in range(4):
            at = slice(16 * r, 16 * r + 16)
            for k in range(3):
                sa[4 * r + k] = gda[at, k * third:(k + 1) * third].astype(BF16)
            sa[4 * r + 3, :, :d_local] = (SCALE * dsec[at]).astype(BF16)
        first_dp[0]()

    def second_gradients():
        low_share(lowa, 28)
        wait_bytes(lowa.at[0:half], red_sem.at[31])
        for q in range(CHUNKS):
            lowta[q] = jnp.transpose(lowa[q * rows:(q + 1) * rows].astype(F32)).astype(BF16)

        def body(q, carry):
            at = pl.ds(pl.multiple_of(q * rows, 16), rows)
            gs[...] += dot_nn(lowta[q, :rank], gg[at])
            us[...] += dot_nn(lowta[q, rank:], ug[at])
            return carry

        lax.fori_loop(0, CHUNKS, body, 0)

    def post(q):
        here = slice(q * rows, (q + 1) * rows)
        lowq = lowb[here]
        width = f_local // 3

        def body(i, carry):
            cols = pl.ds(pl.multiple_of(i * width, 128), width)
            grad = acc[q, :, cols] + dot_nn(lowq, wf[3 * rank:5 * rank, cols])
            gg[here, cols] = (grad * usl[q, :, cols]).astype(BF16)
            ug[here, cols] = (grad * act[q, :, cols]).astype(BF16)
            return carry

        lax.fori_loop(0, 3, body, 0)
        bp[here] = dot_nt(gg[here], wf[:2 * rank]) + dot_nt(ug[here], wf[rank:3 * rank])
        if q == CHUNKS - 2:
            backs[0]()
        if q == CHUNKS - 1:
            last_scatter()

    events = travel_order(hops)
    arrivals = [e for e in events if e[0] > 0]
    count = len(arrivals)
    def take(hop, q):
        for s in range(q * PIECES, (q + 1) * PIECES):
            for b in range(2 if 0 < hop < hops else 1 if hop else 0):
                pair_wait(hop, b, s)
        multiply(hop, q)

    def last_own():
        wait_bytes(wv, w_sem)

    tasks = [(1, last_own)]
    tasks += list(zip(LOW_AT, [
        low_near, low_far, low_sum, lambda: low_share(lowb, 32), use_lows, first_dp[1], lambda: low_spread(lowa, 28)]))
    done = 0
    finished = {}
    for e in events:
        hop, b, s = e
        done += hop > 0
        finished[hop, s // PIECES] = done
    lows_at = LOW_AT[4]
    for (hop, q), at in finished.items():
        ready = at + 1 if hop == 0 else at + LAG
        tasks.append((ready, functools.partial(take, hop, q)))
        if hop == hops:
            ready = max(finished[h, q] for h in range(hops + 1)) + LAG
            at = max(ready, lows_at) + 1 + q if q < CHUNKS - 1 else max(ready, lows_at + CHUNKS, count) + 1
            tasks.append((at, functools.partial(post, q)))
            if q == CHUNKS - 2:
                tasks.append((at + 3, backs[1]))
    tasks.sort(key=lambda t: t[0])

    for q in range(PIECES):
        ring_on(0, 0, q)
    for q in range(CHUNKS * PIECES):
        pair_on(0, 0, q)
    done, first = 0, True
    for hop, b, s in events:
        if hop == 0:
            if b == 1:
                pair_wait(0, 0, s)
            if b == 1 or s >= PIECES:
                ring_on(0, b, s)
            continue
        if first:
            for copy in loads[1:]:
                copy.wait()
            for copy in w_loads:
                copy.start()
            for n in range(CHUNKS):
                prepare(n)
            low_exchange()
            first = False
        ring_wait(hop, b, s)
        if hop + 1 < hops or (hop + 1 == hops and b == 0):
            ring_on(hop, b, s)
        pair_on(hop, b, s)
        done += 1
        if tasks and tasks[0][0] <= done:
            tasks.pop(0)[1]()
    while tasks:
        tasks.pop(0)[1]()

    backs[2]()
    second_gradients()
    for r in range(4):
        at = slice(16 * r, 16 * r + 16)
        for k, full in ((0, gs), (2, us)):
            sb[4 * r + k] = (SCALE * full[at, :640]).astype(BF16)
            sb[4 * r + k + 1, :, :f_local - 640] = (SCALE * full[at, 640:]).astype(BF16)
    second_dp[0]()
    last_gather()
    backs[3]()
    backs[4]()
    back_t = jnp.transpose(bk[:early].astype(F32)).astype(BF16)
    firsts = dot_nn(back_t, xin[:early])
    last_finish()
    back_t = jnp.transpose(bk[early:].astype(F32)).astype(BF16)
    firsts = SCALE * (firsts + dot_nn(back_t, xin[early:]))
    for r in range(4):
        for k in range(2):
            for m in range(2):
                sc[4 * r + 2 * k + m] = firsts[
                    k * rank + 16 * r:k * rank + 16 * r + 16, 128 * m:128 * m + 128].astype(BF16)
    third_dp[0]()
    second_dp[1]()
    low_drain()
    backs[5]()
    last_drain()
    wait_bytes(cg.at[0:2 * hops - 1], ring_send)
    wait_bytes(cg.at[0:2 * hops], pair_send)
    third_dp[1]()
    first_dp[2]()
    second_dp[2]()
    third_dp[2]()


def unpack_kernel(a_ref, b_ref, c_ref, gf, gs, uf, us, gda, dsec):
    f_local = gs.shape[1]
    d_local = gf.shape[1]
    third = f_local // 3
    for r in range(4):
        at = slice(16 * r, 16 * r + 16)
        for k in range(3):
            gda[at, k * third:(k + 1) * third] = a_ref[4 * r + k].astype(F32)
        dsec[at] = a_ref[4 * r + 3, :, :d_local].astype(F32)
        for k, full in ((0, gs), (2, us)):
            full[at, :640] = b_ref[4 * r + k].astype(F32)
            full[at, 640:] = b_ref[4 * r + k + 1, :, :f_local - 640].astype(F32)
        for k, full in ((0, gf), (2, uf)):
            full[at, :128] = c_ref[4 * r + k].astype(F32)
            full[at, 128:] = c_ref[4 * r + k + 1].astype(F32)


def local(nz, nd, inputs, cotangent, gate_pre, up_pre, down_weight, gate_a, gate_b, up_a, up_b, down_a, down_second):
    tokens, d_local = inputs.shape
    f_local = gate_pre.shape[1]
    rank = gate_b.shape[0]
    nt, hops = 2 * nz, nz // 2
    rows, half = tokens // CHUNKS, tokens // 2
    part, group = half // nz, 16 // nd
    wide_a, wide_b, wide_c = f_local // 3, 640, 128
    any_space = pl.BlockSpec(memory_space=pl.ANY)
    vmem, dma = pltpu.VMEM, pltpu.SemaphoreType.DMA

    def dp_buffers(width):
        return [vmem((16, 16, width), BF16), vmem((nd - 1, group, 16, width), BF16), vmem((group, 16, width), BF16)]

    early, wide_low, wide_back = tokens - rows, 4 * rank, 2 * rank
    spread = early // nt

    scratch = [
        vmem((nt, tokens, d_local), BF16),
        vmem((nt, f_local, d_local), BF16),
        vmem((tokens, f_local), BF16),
        vmem((tokens, f_local), BF16),
        vmem((CHUNKS, rows, f_local), F32),
        vmem((CHUNKS, rows, f_local), F32),
        vmem((tokens, f_local), BF16),
        vmem((tokens, d_local), BF16),
        vmem((6 * rank, f_local), BF16),
        vmem((4 * rank, d_local), BF16),
        vmem((CHUNKS, rows, f_local), F32),
        vmem((tokens, wide_low), F32),
        vmem((half, wide_low), F32),
        vmem((5, part, wide_back), BF16),
        vmem((5, part, wide_back), BF16),
        vmem((2, part, wide_back), BF16),
        vmem((2, part, wide_back), BF16),
        vmem((5, part, wide_back), F32),
        vmem((5, part, wide_back), F32),
        vmem((2, part, wide_back), F32),
        vmem((2, part, wide_back), F32),
        vmem((tokens, wide_back), BF16),
        vmem((tokens, wide_back), BF16),
        vmem((CHUNKS, wide_back, rows), BF16),
        vmem((CHUNKS, wide_back, rows), BF16),
        vmem((tokens, wide_back), F32),
        vmem((early // 2, wide_back), F32),
        vmem((nz, spread, wide_back), BF16),
        vmem((nz - 1, spread, wide_back), BF16),
        vmem((nt, rows // nt, wide_back), BF16),
        vmem((nt - 1, rows // nt, wide_back), BF16),
        vmem((tokens, wide_back), BF16),
        vmem((rank, f_local), F32),
        vmem((rank, f_local), F32),
        vmem((rank, f_local), F32),
        vmem((rank, d_local), F32),
        vmem((tokens, f_local), BF16),
        vmem((tokens, f_local), BF16),
        *dp_buffers(wide_a),
        *dp_buffers(wide_b),
        *dp_buffers(wide_c),
        dma((10,)),
        dma,
        dma((2 * hops - 1, CHUNKS * PIECES)),
        dma((2 * hops, CHUNKS * PIECES)),
        dma,
        dma,
        dma((36,)),
        dma((12,)),
        dma((3,)),
    ]
    packed = pl.pallas_call(
        functools.partial(main_kernel, nz, nd),
        out_shape=[jax.ShapeDtypeStruct((16, 16, w), BF16) for w in (wide_a, wide_b, wide_c)],
        in_specs=[any_space] * 11,
        out_specs=[any_space] * 3,
        scratch_shapes=scratch,
        compiler_params=pltpu.CompilerParams(
            collective_id=0, has_side_effects=True, vmem_limit_bytes=56 * 1024 * 1024),
        name="adapters",
    )(inputs, cotangent, gate_pre, up_pre, down_weight, gate_a.T, gate_b, up_a.T, up_b, down_a.T, down_second)
    small = jax.ShapeDtypeStruct((rank, d_local), F32)
    large = jax.ShapeDtypeStruct((rank, f_local), F32)
    gf, gs, uf, us, gda, dsec = pl.pallas_call(
        unpack_kernel, out_shape=[small, large, small, large, large, small], name="unpack")(*packed)
    return gf.T, gs, uf.T, us, gda.T, dsec


def solution(mesh):
    split, rows, columns = P("dp", "tensor"), P("tensor", None), P(None, "tensor")
    return jax.shard_map(
        functools.partial(local, mesh.shape["tensor"] // 2, mesh.shape["dp"]),
        mesh=mesh,
        in_specs=(split, split, split, split, rows, rows, columns, rows, columns, rows, columns),
        out_specs=(rows, columns, rows, columns, rows, columns),
        check_vma=False,
    )
```
